256 devices in a mesh: rep: 32 (over x, z_hi, y), fsdp: 8 (over z_lo, core).
Axes of the slice: x: 4, y: 4, z: 8 (z_hi: 2, z_lo: 4; z = z_hi * 4 + z_lo), core: 2. Of those that a mesh axis runs over, the one named last changes fastest.
Arguments:
- tokens: bfloat16 [32, 2048, 4096], P('rep', 'fsdp'), may hold values from -90 to 90
- cotangent: bfloat16 [32, 2048, 2048], P('rep', 'fsdp'), may hold values from -6 to 6
- w_slow: bfloat16 [32, 4096, 2048], P('rep', 'fsdp'), may hold values from -6 to 6
- drift: bfloat16 [32, 4096, 2048], P('rep', 'fsdp'), may hold values from -4 to 4
- momentum: bfloat16 [32, 4096, 2048], P('rep', 'fsdp'), may hold values from -4 to 4
- partner: int32 [32], replicated, may hold values from 0 to 31, as said below
Outputs:
- momentum_new: bfloat16 [32, 4096, 2048], P('rep', 'fsdp')
- weights_new: bfloat16 [32, 4096, 2048], P('rep', 'fsdp')
The draws below stay inside these ranges and needn't reach their ends.
Inputs may be any that keep to these rules, and one draw needn't show every extreme that they name: partner[partner[r]] == r and partner[r] != r for every replica r.
All inputs are finite; a program needn't handle non-finite values.
Results may differ from the reference program's by a relative error of at most 0.013.
Values may be sent and summed in bfloat16 or wider, within the bound.
No kernel may reach another device: no remote copies, remote signals or barrier semaphores. Data moves between devices by JAX's collectives and lax.ppermute only.
A program may use at most 128 MiB of HBM per device.

```python
import math
import jax
import jax.numpy as jnp
from jax import lax

D = 4096
DO = 2048
TOK_DEV = 256
TOK_REP = 2048
REPLICAS = 32
N_REP = 32
N_FSDP = 8


def draw_tokens(key, part):
    key = jax.random.fold_in(key, 11)
    first, second = jax.random.split(key)
    column = jnp.arange(D, dtype=jnp.float32) / D
    rising = jnp.exp(math.log(10.0) * column)
    base = jax.random.truncated_normal(first, -6.0, 6.0, (REPLICAS, TOK_REP, D), jnp.float32)
    factor = jnp.exp(jax.random.uniform(second, (D,), jnp.float32, math.log(0.7), math.log(1.4)))
    return (base * rising * factor).astype(jnp.bfloat16)


def draw_partner(key, part):
    key = jax.random.fold_in(key, 23)
    order = jax.random.permutation(key, REPLICAS).astype(jnp.int32)
    flipped = order.reshape(REPLICAS // 2, 2)[:, ::-1].reshape(REPLICAS)
    return jnp.zeros((REPLICAS,), jnp.int32).at[order].set(flipped)


def block_levels(rng, shape, cuts, low, high):
    gain, own = 1.0, jax.random.fold_in(rng, 6)
    for axis_at, blocks in cuts:
        steps = jnp.exp(jax.random.uniform(jax.random.fold_in(own, axis_at), (blocks,), jnp.float32, low / len(cuts), high / len(cuts)))
        gain = gain * jnp.repeat(steps, shape[axis_at] // blocks).reshape([-1 if axis == axis_at else 1 for axis in range(len(shape))])
    return gain


def noise(key, shape, deviation, limit, cuts=(), held_as=jnp.bfloat16):
    loudness = block_levels(key, shape, cuts, -0.22, 0.18) if cuts else 1.0
    drawn = jax.random.normal(key, shape, jnp.float32) * deviation * loudness
    return jnp.minimum(jnp.maximum(drawn, -limit), limit).astype(held_as)


def setup_inputs(seed: int = 0) -> dict:
    arg_keys = jax.random.split(jax.random.key(seed), 7)
    return {
        "tokens": draw_tokens(jax.random.fold_in(arg_keys[6], 71), 0),
        "cotangent": noise(arg_keys[1], (REPLICAS, TOK_REP, DO), 1.0, 6.0, ((0, 32), (1, 8))),
        "w_slow": noise(arg_keys[2], (REPLICAS, D, DO), 1.0, 6.0, ((0, 32), (1, 8))),
        "drift": noise(arg_keys[3], (REPLICAS, D, DO), 0.5, 4.0, ((0, 32), (1, 8))),
        "momentum": noise(arg_keys[4], (REPLICAS, D, DO), 0.5, 4.0, ((0, 32), (1, 8))),
        "partner": draw_partner(jax.random.fold_in(arg_keys[6], 71), 0),
    }


def one_replica(index, tokens, cotangent, w_slow, drift, momentum, partner):
    token_blocks = tokens[index].astype(jnp.float32).reshape(N_FSDP, TOK_DEV, D)
    grad_blocks = cotangent[index].astype(jnp.float32).reshape(N_FSDP, TOK_DEV, DO)

    def add_block(total, pair):
        block_x, block_g = pair
        partial_sum = jnp.dot(block_x.T, block_g, precision=lax.Precision.HIGHEST)
        rounded = lax.optimization_barrier(partial_sum.astype(jnp.bfloat16))
        return (total + rounded.astype(jnp.float32), None)
    grad, unused = lax.scan(add_block, jnp.zeros((D, DO), jnp.float32), (token_blocks, grad_blocks))
    scale = jnp.sqrt(jnp.mean(grad * grad) + 1e-06)
    mate = partner[index]
    partner_mix = (0.5 * (0.7 * drift[mate].astype(jnp.float32) - 0.3 * w_slow[mate].astype(jnp.float32))).astype(jnp.bfloat16)
    own_slow = w_slow[index].astype(jnp.float32)
    moment = 0.5 * momentum[index].astype(jnp.float32) + 0.35 * drift[index].astype(jnp.float32) + 0.15 * own_slow + partner_mix.astype(jnp.float32)
    weights = own_slow - moment - 0.5 * grad / scale
    return (moment.astype(jnp.bfloat16), weights.astype(jnp.bfloat16))

def reference(tokens, cotangent, w_slow, drift, momentum, partner):

    def step(index):
        return one_replica(index, tokens, cotangent, w_slow, drift, momentum, partner)
    momentum_new, weights_new = lax.map(step, jnp.arange(N_REP, dtype=jnp.int32))
    return (momentum_new, weights_new)
```

```python
import jax
import jax.numpy as jnp
from jax import lax
from jax.sharding import PartitionSpec as P

NX, NH, NY = 4, 2, 4
N_PLANE = NX * NY
N_FSDP = 8


def replica_at(spot, half):
    return (spot // NY * NH + half) * NY + spot % NY


PLANES = [[replica_at(spot, half) for spot in range(N_PLANE)] for half in range(NH)]
ACROSS = [
    (replica_at(spot, half), replica_at(spot, 1 - half))
    for spot in range(N_PLANE)
    for half in range(NH)
]


def mixing_term(drift_part, slow_part):
    return (
        0.5 * (0.7 * drift_part.astype(jnp.float32) - 0.3 * slow_part.astype(jnp.float32))
    ).astype(jnp.bfloat16)


def plane_plan(partner, half):
    spots = jnp.arange(N_PLANE, dtype=jnp.int32)
    mate = partner[replica_at(spots, half)]
    mate_spot = mate // (NH * NY) * NY + mate % NY
    crosses = mate // NY % NH != half
    place = jnp.cumsum(crosses.astype(jnp.int32)) - 1
    return mate_spot, crosses, place


def exchange_mix(mix, partner):
    rows, cols = mix.shape
    half = lax.axis_index("rep") // NY % NH
    held = lax.all_to_all(
        mix.reshape(N_PLANE, rows // N_PLANE, cols),
        "rep",
        split_axis=0,
        concat_axis=0,
        tiled=True,
        axis_index_groups=PLANES,
    )
    mate_spot, crosses, place = plane_plan(partner, half)
    far_spot, far_crosses, far_place = plane_plan(partner, 1 - half)
    slots = jnp.arange(N_PLANE, dtype=jnp.int32)
    wanted = jnp.sum(
        jnp.where(
            far_crosses[None, :] & (far_place[None, :] == slots[:, None]), far_spot[None, :], 0
        ),
        axis=1,
    )
    outgoing = jnp.take(held, wanted, axis=0, mode="clip")
    count = jnp.sum(crosses.astype(jnp.int32))

    def swap(width):
        def branch(block):
            if width == 0:
                return block
            moved = lax.ppermute(block[:width], "rep", ACROSS)
            return jnp.concatenate([moved, block[width:]], axis=0)

        return branch

    arrived = lax.switch(
        (count + 1) // 2, [swap(2 * n) for n in range(N_PLANE // 2 + 1)], outgoing
    )
    pool = jnp.concatenate([held, arrived], axis=0)
    routed = jnp.take(pool, jnp.where(crosses, N_PLANE + place, mate_spot), axis=0, mode="clip")
    back = lax.all_to_all(
        routed, "rep", split_axis=0, concat_axis=0, tiled=True, axis_index_groups=PLANES
    )
    return back.reshape(rows, cols)


def gather_tokens(local_x):
    block, width = local_x.shape[0], local_x.shape[1] // N_FSDP
    me = lax.axis_index("fsdp")
    out = jnp.zeros((N_FSDP, block, width), local_x.dtype)
    for step in range(N_FSDP):
        piece = lax.dynamic_slice_in_dim(local_x, (me + step) % N_FSDP * width, width, axis=1)
        if step:
            piece = lax.ppermute(
                piece, "fsdp", [(i, (i + step) % N_FSDP) for i in range(N_FSDP)]
            )
        out = lax.dynamic_update_index_in_dim(out, piece, (me - step) % N_FSDP, axis=0)
    return out.reshape(N_FSDP * block, width)


def on_device(tokens, cotangent, w_slow, drift, momentum, partner):
    all_g = lax.all_gather(cotangent[0], "fsdp", axis=0, tiled=True)
    own_x = gather_tokens(tokens[0])
    partner_mix = exchange_mix(mixing_term(drift[0], w_slow[0]), partner)
    grad = lax.dot_general(
        own_x, all_g, (((0,), (0,)), ((), ())), preferred_element_type=jnp.float32
    )
    squares = lax.psum(jnp.sum(grad * grad), "fsdp")
    scale = jnp.sqrt(squares / (grad.shape[0] * N_FSDP * grad.shape[1]) + 1e-06)
    own_slow = w_slow[0].astype(jnp.float32)
    moment = (
        0.5 * momentum[0].astype(jnp.float32)
        + 0.35 * drift[0].astype(jnp.float32)
        + 0.15 * own_slow
        + partner_mix.astype(jnp.float32)
    )
    weights = own_slow - moment - 0.5 * (grad / scale)
    return (moment.astype(jnp.bfloat16)[None], weights.astype(jnp.bfloat16)[None])


def solution(mesh):
    return jax.shard_map(
        on_device,
        mesh=mesh,
        in_specs=(
            P("rep", "fsdp", None),
            P("rep", "fsdp", None),
            P("rep", "fsdp", None),
            P("rep", "fsdp", None),
            P("rep", "fsdp", None),
            P(),
        ),
        out_specs=(P("rep", "fsdp", None), P("rep", "fsdp", None)),
        check_vma=False,
    )
```

```python
import jax
import jax.numpy as jnp
from jax import lax
from jax.experimental import pallas as pl
from jax.experimental.pallas import tpu as pltpu
from jax.sharding import PartitionSpec as P

NX, NH, NY = 4, 2, 4
N_PLANE = NX * NY
N_CHIP, N_CORE = 4, 2
N_FSDP = N_CHIP * N_CORE


def replica_at(spot, half):
    return (spot // NY * NH + half) * NY + spot % NY


PLANES = [[replica_at(spot, half) for spot in range(N_PLANE)] for half in range(NH)]
ACROSS = [
    (replica_at(spot, half), replica_at(spot, 1 - half))
    for spot in range(N_PLANE)
    for half in range(NH)
]


def between_chips(pairs):
    return [
        (src * N_CORE + core, dst * N_CORE + core) for src, dst in pairs for core in range(N_CORE)
    ]


ENDS_SWAP = between_chips([(0, 1), (1, 0), (2, 3), (3, 2)])
MID_SWAP = between_chips([(1, 2), (2, 1)])
MID_TO_ENDS = between_chips([(1, 0), (2, 3)])
SIBLING = [(i, i ^ 1) for i in range(N_FSDP)]


def chips_apart(step):
    return between_chips([(i, i ^ step) for i in range(N_CHIP)])


WIDTHS = (4, 6, 8, 10, 12, 16)


def mixing_term(drift, w_slow):
    def kernel(drift_ref, slow_ref, out_ref):
        out_ref[...] = (
            0.5
            * (
                0.7 * drift_ref[...].astype(jnp.float32)
                - 0.3 * slow_ref[...].astype(jnp.float32)
            )
        ).astype(jnp.bfloat16)

    rows, cols = drift.shape
    tile = pl.BlockSpec((rows // 4, cols), lambda i: (i, 0))
    return pl.pallas_call(
        kernel,
        grid=(4,),
        out_shape=jax.ShapeDtypeStruct(drift.shape, drift.dtype),
        in_specs=[tile, tile],
        out_specs=tile,
        compiler_params=pltpu.CompilerParams(vmem_limit_bytes=48 << 20),
    )(drift, w_slow)


def route(held, moved, pick):
    def kernel(pick_ref, held_ref, moved_ref, out_ref, sems):
        for spot in range(N_PLANE):
            at = pick_ref[spot]

            @pl.when(at < N_PLANE)
            def _():
                pltpu.make_async_copy(
                    held_ref.at[jnp.minimum(at, N_PLANE - 1)], out_ref.at[spot], sems.at[spot]
                ).start()

            @pl.when(at >= N_PLANE)
            def _():
                from_far = jnp.clip(at - N_PLANE, 0, moved_ref.shape[0] - 1)
                pltpu.make_async_copy(
                    moved_ref.at[from_far], out_ref.at[spot], sems.at[spot]
                ).start()

        for spot in range(N_PLANE):
            pltpu.make_async_copy(held_ref.at[0], out_ref.at[spot], sems.at[spot]).wait()

    return pl.pallas_call(
        kernel,
        out_shape=jax.ShapeDtypeStruct(held.shape, held.dtype),
        in_specs=[
            pl.BlockSpec(memory_space=pltpu.SMEM),
            pl.BlockSpec(memory_space=pltpu.VMEM),
            pl.BlockSpec(memory_space=pltpu.VMEM),
        ],
        out_specs=pl.BlockSpec(memory_space=pl.ANY),
        scratch_shapes=[pltpu.SemaphoreType.DMA((N_PLANE,))],
        compiler_params=pltpu.CompilerParams(vmem_limit_bytes=48 << 20),
        cost_estimate=pl.CostEstimate(
            flops=0, bytes_accessed=200 * held.size, transcendentals=0
        ),
    )(pick, held, moved)


def plane_plan(partner, half):
    spots = jnp.arange(N_PLANE, dtype=jnp.int32)
    mate = partner[replica_at(spots, half)]
    mate_spot = mate // (NH * NY) * NY + mate % NY
    crosses = mate // NY % NH != half
    place = jnp.cumsum(crosses.astype(jnp.int32)) - 1
    return mate_spot, crosses, place


def in_plane(blocks):
    return lax.all_to_all(
        blocks, "rep", split_axis=0, concat_axis=0, tiled=True, axis_index_groups=PLANES
    )


def add_products(acc, pairs, square):
    rows, cols = pairs[0][0].shape[1], pairs[0][1].shape[1]
    tile = 512
    flat = [part for pair in pairs for part in pair]
    n_acc = acc is not None

    def kernel(*refs):
        ins, outs = refs[: n_acc + len(flat)], refs[n_acc + len(flat) :]
        total = ins[0][...] if n_acc else None
        at = n_acc
        for x, *gs in pairs:
            g = ins[at + 1][...]
            for k in range(1, len(gs)):
                g = g + ins[at + 1 + k][...]
            part = lax.dot_general(
                ins[at][...], g, (((0,), (0,)), ((), ())), preferred_element_type=jnp.float32
            )
            total = part if total is None else total + part
            at += 1 + len(gs)
        outs[0][...] = total
        if square:
            sums = jnp.sum((total * total).reshape(rows // 8, 8, tile), axis=0)
            sums = sum(sums[:, k * 128 : (k + 1) * 128] for k in range(tile // 128))

            @pl.when(pl.program_id(0) == 0)
            def _():
                outs[1][...] = sums

            @pl.when(pl.program_id(0) > 0)
            def _():
                outs[1][...] += sums

    wide = pl.BlockSpec((rows, tile), lambda i: (0, i))
    specs = [wide] * n_acc
    for x, *gs in pairs:
        specs.append(pl.BlockSpec(x.shape, lambda i: (0, 0)))
        specs += [pl.BlockSpec((g.shape[0], tile), lambda i: (0, i)) for g in gs]
    out_shape = [jax.ShapeDtypeStruct((rows, cols), jnp.float32)]
    out_specs = [wide]
    if square:
        out_shape.append(jax.ShapeDtypeStruct((8, 128), jnp.float32))
        out_specs.append(pl.BlockSpec((8, 128), lambda i: (0, 0)))
    return pl.pallas_call(
        kernel,
        grid=(cols // tile,),
        out_shape=out_shape,
        in_specs=specs,
        out_specs=out_specs,
        compiler_params=pltpu.CompilerParams(vmem_limit_bytes=48 << 20),
        cost_estimate=pl.CostEstimate(
            flops=0,
            bytes_accessed=rows * cols,
            transcendentals=0,
        ),
    )(*([acc] if n_acc else []), *flat)


def outer_step(momentum, drift, w_slow, mix, grad, squares, count):
    n_squares = len(squares)

    def kernel(momentum_ref, drift_ref, slow_ref, mix_ref, grad_ref, *refs):
        total = refs[0][...]
        for ref in refs[1:n_squares]:
            total = total + ref[...]
        total = jnp.sum(jnp.sum(total, axis=0, keepdims=True), axis=1, keepdims=True)
        factor = 0.5 / jnp.sqrt(total / count + 1e-06)
        moment_ref, weights_ref = refs[n_squares:]
        slow = slow_ref[...].astype(jnp.float32)
        moment = (
            0.5 * momentum_ref[...].astype(jnp.float32)
            + 0.35 * drift_ref[...].astype(jnp.float32)
            + 0.15 * slow
            + mix_ref[...].astype(jnp.float32)
        )
        moment_ref[...] = moment.astype(jnp.bfloat16)
        weights_ref[...] = (slow - moment - grad_ref[...] * factor).astype(jnp.bfloat16)

    rows, cols = grad.shape
    tile = pl.BlockSpec((rows // 8, cols), lambda i: (i, 0))
    whole = pl.BlockSpec((8, 128), lambda i: (0, 0))
    return pl.pallas_call(
        kernel,
        grid=(8,),
        out_shape=[jax.ShapeDtypeStruct(grad.shape, jnp.bfloat16)] * 2,
        in_specs=[tile] * 5 + [whole] * n_squares,
        out_specs=[tile] * 2,
        compiler_params=pltpu.CompilerParams(vmem_limit_bytes=48 << 20),
        cost_estimate=pl.CostEstimate(
            flops=12 * grad.size, bytes_accessed=16 * grad.size, transcendentals=0
        ),
    )(momentum, drift, w_slow, mix, grad, *squares)


def on_device(tokens, cotangent, w_slow, drift, momentum, partner):
    local_x, local_g = tokens[0], cotangent[0]
    rows, cols = w_slow.shape[1:]
    half = lax.axis_index("rep") // NY % NH
    me = lax.axis_index("fsdp")
    chip, core = me // N_CORE, me % N_CORE

    def hop(x, pairs):
        return lax.ppermute(x, "fsdp", pairs)

    def to_sibling(x):
        return hop(x, SIBLING)

    def columns_from(step):
        span = N_CORE * rows
        x = lax.dynamic_slice_in_dim(local_x, (chip ^ step) * span, span, axis=1)
        return hop(x, chips_apart(step)) if step else x

    def halves(x):
        own = lax.dynamic_slice_in_dim(x, core * rows, rows, axis=1)
        other = lax.dynamic_slice_in_dim(x, (1 - core) * rows, rows, axis=1)
        return own, to_sibling(other)

    mate_spot, crosses, place = plane_plan(partner, half)
    far_spot, far_crosses, far_place = plane_plan(partner, 1 - half)
    slots = jnp.arange(N_PLANE, dtype=jnp.int32)
    wanted = jnp.sum(
        jnp.where(
            far_crosses[None, :] & (far_place[None, :] == slots[:, None]), far_spot[None, :], 0
        ),
        axis=1,
    )
    pick = jnp.where(crosses, N_PLANE + place, mate_spot)
    count = jnp.sum(crosses.astype(jnp.int32))
    case = sum((count > width).astype(jnp.int32) for width in WIDTHS[:-1])
    g_near = hop(local_g, ENDS_SWAP)
    g_mid = hop(local_g, MID_SWAP)
    near_x = [columns_from(step) for step in range(3)]
    mix = mixing_term(drift[0], w_slow[0])
    held = in_plane(mix.reshape(N_PLANE, rows // N_PLANE, cols))
    held, g_near, g_mid, near_x = lax.optimization_barrier((held, g_near, g_mid, near_x))

    g_ends = hop(g_mid, MID_TO_ENDS)
    g_far = hop(g_near, MID_SWAP)

    def cross(width):
        def branch(held):
            sent = jnp.take(held, wanted[:width], axis=0, mode="clip")
            routed = route(held, lax.ppermute(sent, "rep", ACROSS), pick)
            return routed

        return branch

    routed = lax.switch(
        case, [cross(width) for width in WIDTHS], held
    )

    g_last = hop(g_far, MID_TO_ENDS)
    last_x = [
        hop(
            lax.dynamic_slice_in_dim(local_x, (me ^ step) * rows, rows, axis=1),
            [(i, i ^ step) for i in range(N_FSDP)],
        )
        for step in (6, 7)
    ]
    partner_mix = in_plane(routed).reshape(rows, cols)
    xs = [halves(x) for x in near_x]
    (acc,) = add_products(
        None,
        [
            (xs[0][0], local_g),
            (xs[0][1], to_sibling(local_g)),
            (xs[1][0], g_near),
            (xs[1][1], to_sibling(g_near)),
            (xs[2][0], g_ends, g_far),
            (xs[2][1], to_sibling(g_ends), to_sibling(g_far)),
        ],
        False,
    )
    sib_mid = to_sibling(g_mid)
    g_last, last_x, acc, sib_mid = lax.optimization_barrier((g_last, last_x, acc, sib_mid))
    grad, squares = add_products(
        acc,
        [(last_x[0], g_mid, g_last), (last_x[1], sib_mid, to_sibling(g_last))],
        True,
    )
    squares = squares + to_sibling(squares)
    others = [hop(squares, chips_apart(step)) for step in (1, 2, 3)]
    moment, weights = outer_step(
        momentum[0],
        drift[0],
        w_slow[0],
        partner_mix,
        grad,
        [squares] + others,
        rows * N_FSDP * cols,
    )
    return (moment[None], weights[None])


def solution(mesh):
    return jax.shard_map(
        on_device,
        mesh=mesh,
        in_specs=(
            P("rep", "fsdp", None),
            P("rep", "fsdp", None),
            P("rep", "fsdp", None),
            P("rep", "fsdp", None),
            P("rep", "fsdp", None),
            P(),
        ),
        out_specs=(P("rep", "fsdp", None), P("rep", "fsdp", None)),
        check_vma=False,
    )
```

```python
import jax
import jax.numpy as jnp
from jax import lax
from jax.experimental import pallas as pl
from jax.experimental.pallas import tpu as pltpu
from jax.sharding import PartitionSpec as P

NX, NH, NY = 4, 2, 4
N_PLANE = NX * NY
N_CHIP, N_CORE = 4, 2
N_FSDP = N_CHIP * N_CORE


def replica_at(spot, half):
    return (spot // NY * NH + half) * NY + spot % NY


PLANES = [[replica_at(spot, half) for spot in range(N_PLANE)] for half in range(NH)]
ACROSS = [
    (replica_at(spot, half), replica_at(spot, 1 - half))
    for spot in range(N_PLANE)
    for half in range(NH)
]


def between_chips(pairs):
    return [
        (src * N_CORE + core, dst * N_CORE + core) for src, dst in pairs for core in range(N_CORE)
    ]


ENDS_SWAP = between_chips([(0, 1), (1, 0), (2, 3), (3, 2)])
MID_SWAP = between_chips([(1, 2), (2, 1)])
MID_TO_ENDS = between_chips([(1, 0), (2, 3)])
SIBLING = [(i, i ^ 1) for i in range(N_FSDP)]


def chips_apart(step):
    return between_chips([(i, i ^ step) for i in range(N_CHIP)])


WIDTHS = (4, 6, 8, 10, 12, 16)


def by_chunks(ref, body):
    @pl.loop(0, ref.shape[0] // 16)
    def _(i):
        for col in range(0, ref.shape[1], 512):
            body((pl.ds(pl.multiple_of(i * 16, 16), 16), pl.ds(col, 512)))


def mixing_term(drift, w_slow):
    def kernel(drift_ref, slow_ref, out_ref):
        def chunk(at):
            out_ref[at] = (
                0.5
                * (
                    0.7 * drift_ref[at].astype(jnp.float32)
                    - 0.3 * slow_ref[at].astype(jnp.float32)
                )
            ).astype(jnp.bfloat16)

        by_chunks(out_ref, chunk)

    rows, cols = drift.shape
    tile = pl.BlockSpec((rows // 4, cols), lambda i: (i, 0))
    return pl.pallas_call(
        kernel,
        grid=(4,),
        out_shape=jax.ShapeDtypeStruct(drift.shape, drift.dtype),
        in_specs=[tile, tile],
        out_specs=tile,
        compiler_params=pltpu.CompilerParams(vmem_limit_bytes=14 << 20),
    )(drift, w_slow)


def route(held, moved, pick):
    def kernel(pick_ref, held_ref, moved_ref, out_ref, sems):
        for spot in range(N_PLANE):
            at = pick_ref[spot]

            @pl.when(at < N_PLANE)
            def _():
                pltpu.make_async_copy(
                    held_ref.at[jnp.minimum(at, N_PLANE - 1)], out_ref.at[spot], sems.at[spot]
                ).start()

            @pl.when(at >= N_PLANE)
            def _():
                from_far = jnp.clip(at - N_PLANE, 0, moved_ref.shape[0] - 1)
                pltpu.make_async_copy(
                    moved_ref.at[from_far], out_ref.at[spot], sems.at[spot]
                ).start()

        for spot in range(N_PLANE):
            pltpu.make_async_copy(held_ref.at[0], out_ref.at[spot], sems.at[spot]).wait()

    return pl.pallas_call(
        kernel,
        out_shape=jax.ShapeDtypeStruct(held.shape, held.dtype),
        in_specs=[
            pl.BlockSpec(memory_space=pltpu.SMEM),
            pl.BlockSpec(memory_space=pltpu.VMEM),
            pl.BlockSpec(memory_space=pltpu.VMEM),
        ],
        out_specs=pl.BlockSpec(memory_space=pl.ANY),
        scratch_shapes=[pltpu.SemaphoreType.DMA((N_PLANE,))],
        compiler_params=pltpu.CompilerParams(vmem_limit_bytes=14 << 20),
        cost_estimate=pl.CostEstimate(
            flops=0, bytes_accessed=200 * held.size, transcendentals=0
        ),
    )(pick, held, moved)


def plane_plan(partner, half):
    spots = jnp.arange(N_PLANE, dtype=jnp.int32)
    mate = partner[replica_at(spots, half)]
    mate_spot = mate // (NH * NY) * NY + mate % NY
    crosses = mate // NY % NH != half
    place = jnp.cumsum(crosses.astype(jnp.int32)) - 1
    return mate_spot, crosses, place


def in_plane(blocks):
    return lax.all_to_all(
        blocks, "rep", split_axis=0, concat_axis=0, tiled=True, axis_index_groups=PLANES
    )


def add_products(acc, pairs, square):
    rows, cols = pairs[0][0].shape[1], pairs[0][1].shape[1]
    tile = 512
    flat = [part for pair in pairs for part in pair]
    n_acc = acc is not None

    def kernel(*refs):
        ins, outs = refs[: n_acc + len(flat)], refs[n_acc + len(flat) :]
        total = ins[0][...] if n_acc else None
        at = n_acc
        for x, *gs in pairs:
            g = ins[at + 1][...]
            for k in range(1, len(gs)):
                g = g + ins[at + 1 + k][...]
            part = lax.dot_general(
                ins[at][...], g, (((0,), (0,)), ((), ())), preferred_element_type=jnp.float32
            )
            total = part if total is None else total + part
            at += 1 + len(gs)
        outs[0][...] = total
        if square:
            sums = jnp.sum((total * total).reshape(rows // 8, 8, tile), axis=0)
            sums = sum(sums[:, k * 128 : (k + 1) * 128] for k in range(tile // 128))

            @pl.when(pl.program_id(0) == 0)
            def _():
                outs[1][...] = sums

            @pl.when(pl.program_id(0) > 0)
            def _():
                outs[1][...] += sums

    wide = pl.BlockSpec((rows, tile), lambda i: (0, i))
    specs = [wide] * n_acc
    for x, *gs in pairs:
        specs.append(pl.BlockSpec(x.shape, lambda i: (0, 0)))
        specs += [pl.BlockSpec((g.shape[0], tile), lambda i: (0, i)) for g in gs]
    out_shape = [jax.ShapeDtypeStruct((rows, cols), jnp.float32)]
    out_specs = [wide]
    if square:
        out_shape.append(jax.ShapeDtypeStruct((8, 128), jnp.float32))
        out_specs.append(pl.BlockSpec((8, 128), lambda i: (0, 0)))
    return pl.pallas_call(
        kernel,
        grid=(cols // tile,),
        out_shape=out_shape,
        in_specs=specs,
        out_specs=out_specs,
        compiler_params=pltpu.CompilerParams(vmem_limit_bytes=14 << 20),
        cost_estimate=pl.CostEstimate(
            flops=0,
            bytes_accessed=rows * cols,
            transcendentals=0,
        ),
    )(*([acc] if n_acc else []), *flat)


def momentum_step(momentum, drift, w_slow, mix):
    def kernel(momentum_ref, drift_ref, slow_ref, mix_ref, moment_ref, base_ref):
        def chunk(at):
            slow = slow_ref[at].astype(jnp.float32)
            moment = (
                0.5 * momentum_ref[at].astype(jnp.float32)
                + 0.35 * drift_ref[at].astype(jnp.float32)
                + 0.15 * slow
                + mix_ref[at].astype(jnp.float32)
            )
            moment_ref[at] = moment.astype(jnp.bfloat16)
            base_ref[at] = slow - moment

        by_chunks(moment_ref, chunk)

    rows, cols = momentum.shape
    tile = pl.BlockSpec((rows // 8, cols), lambda i: (i, 0))
    return pl.pallas_call(
        kernel,
        grid=(8,),
        out_shape=[
            jax.ShapeDtypeStruct(momentum.shape, jnp.bfloat16),
            jax.ShapeDtypeStruct(momentum.shape, jnp.float32),
        ],
        in_specs=[tile] * 4,
        out_specs=[tile] * 2,
        compiler_params=pltpu.CompilerParams(vmem_limit_bytes=14 << 20),
        cost_estimate=pl.CostEstimate(
            flops=0, bytes_accessed=14 * momentum.size, transcendentals=0
        ),
    )(momentum, drift, w_slow, mix)


def weight_step(base, grad, squares, count):
    def kernel(base_ref, grad_ref, *refs):
        total = refs[0][...]
        for ref in refs[1:-1]:
            total = total + ref[...]
        total = jnp.sum(jnp.sum(total, axis=0, keepdims=True), axis=1, keepdims=True)
        factor = 0.5 / jnp.sqrt(total / count + 1e-06)
        factor = jnp.broadcast_to(factor, (16, 512))

        def chunk(at):
            refs[-1][at] = (base_ref[at] - grad_ref[at] * factor).astype(jnp.bfloat16)

        by_chunks(base_ref, chunk)

    rows, cols = base.shape
    tile = pl.BlockSpec((rows // 8, cols), lambda i: (i, 0))
    whole = pl.BlockSpec((8, 128), lambda i: (0, 0))
    return pl.pallas_call(
        kernel,
        grid=(8,),
        out_shape=jax.ShapeDtypeStruct(base.shape, jnp.bfloat16),
        in_specs=[tile] * 2 + [whole] * len(squares),
        out_specs=tile,
        compiler_params=pltpu.CompilerParams(vmem_limit_bytes=14 << 20),
        cost_estimate=pl.CostEstimate(
            flops=3 * base.size, bytes_accessed=10 * base.size, transcendentals=0
        ),
    )(base, grad, *squares)


def after(values, *arrays):
    def kernel(values_ref, *refs):
        for i in range(values.shape[0]):
            refs[-1][i] = values_ref[i]

    return pl.pallas_call(
        kernel,
        out_shape=jax.ShapeDtypeStruct(values.shape, values.dtype),
        in_specs=[pl.BlockSpec(memory_space=pltpu.SMEM)]
        + [pl.BlockSpec(memory_space=pl.ANY)] * len(arrays),
        out_specs=pl.BlockSpec(memory_space=pltpu.SMEM),
        cost_estimate=pl.CostEstimate(flops=3 * 10**9, bytes_accessed=0, transcendentals=0),
    )(values, *arrays)


def on_device(tokens, cotangent, w_slow, drift, momentum, partner):
    local_x, local_g = tokens[0], cotangent[0]
    rows, cols = w_slow.shape[1:]
    half = lax.axis_index("rep") // NY % NH
    me = lax.axis_index("fsdp")
    chip, core = me // N_CORE, me % N_CORE

    def hop(x, pairs):
        return lax.ppermute(x, "fsdp", pairs)

    def to_sibling(x):
        return hop(x, SIBLING)

    def columns_from(step):
        span = N_CORE * rows
        x = lax.dynamic_slice_in_dim(local_x, (chip ^ step) * span, span, axis=1)
        return hop(x, chips_apart(step)) if step else x

    def halves(x):
        own = lax.dynamic_slice_in_dim(x, core * rows, rows, axis=1)
        other = lax.dynamic_slice_in_dim(x, (1 - core) * rows, rows, axis=1)
        return own, to_sibling(other)

    mate_spot, crosses, place = plane_plan(partner, half)
    far_spot, far_crosses, far_place = plane_plan(partner, 1 - half)
    slots = jnp.arange(N_PLANE, dtype=jnp.int32)
    wanted = jnp.sum(
        jnp.where(
            far_crosses[None, :] & (far_place[None, :] == slots[:, None]), far_spot[None, :], 0
        ),
        axis=1,
    )
    pick = jnp.where(crosses, N_PLANE + place, mate_spot)
    count = jnp.sum(crosses.astype(jnp.int32))
    case = sum((count > width).astype(jnp.int32) for width in WIDTHS[:-1])
    g_near = hop(local_g, ENDS_SWAP)
    g_mid = hop(local_g, MID_SWAP)
    near_x = [columns_from(step) for step in range(3)]
    mix = mixing_term(drift[0], w_slow[0])
    held = in_plane(mix.reshape(N_PLANE, rows // N_PLANE, cols))
    wanted = after(wanted, g_near, g_mid, near_x[1], near_x[2])
    plan = (wanted, pick, case)
    held, g_near, g_mid, near_x, plan = lax.optimization_barrier(
        (held, g_near, g_mid, near_x, plan)
    )
    wanted, pick, case = plan

    g_ends = hop(g_mid, MID_TO_ENDS)
    g_far = hop(g_near, MID_SWAP)

    def cross(width):
        def branch(held):
            sent = jnp.take(held, wanted[:width], axis=0, mode="clip")
            routed = route(held, lax.ppermute(sent, "rep", ACROSS), pick)
            return routed

        return branch

    routed = lax.switch(
        case, [cross(width) for width in WIDTHS], held
    )

    g_last = hop(g_far, MID_TO_ENDS)
    last_x = [
        hop(
            lax.dynamic_slice_in_dim(local_x, (me ^ step) * rows, rows, axis=1),
            [(i, i ^ step) for i in range(N_FSDP)],
        )
        for step in (6, 7)
    ]
    partner_mix = in_plane(routed).reshape(rows, cols)
    xs = [halves(x) for x in near_x]
    (acc,) = add_products(
        None,
        [
            (xs[0][0], local_g),
            (xs[0][1], to_sibling(local_g)),
            (xs[1][0], g_near),
            (xs[1][1], to_sibling(g_near)),
            (xs[2][0], g_ends, g_far),
            (xs[2][1], to_sibling(g_ends), to_sibling(g_far)),
        ],
        False,
    )
    sib_mid = to_sibling(g_mid)
    g_last, last_x, acc, sib_mid = lax.optimization_barrier((g_last, last_x, acc, sib_mid))
    grad, squares = add_products(
        acc,
        [(last_x[0], g_mid, g_last), (last_x[1], sib_mid, to_sibling(g_last))],
        True,
    )
    squares = squares + to_sibling(squares)
    others = [hop(squares, chips_apart(step)) for step in (1, 2, 3)]
    moment, base = momentum_step(momentum[0], drift[0], w_slow[0], partner_mix)
    weights = weight_step(base, grad, [squares] + others, rows * N_FSDP * cols)
    return (moment[None], weights[None])


def solution(mesh):
    return jax.shard_map(
        on_device,
        mesh=mesh,
        in_specs=(
            P("rep", "fsdp", None),
            P("rep", "fsdp", None),
            P("rep", "fsdp", None),
            P("rep", "fsdp", None),
            P("rep", "fsdp", None),
            P(),
        ),
        out_specs=(P("rep", "fsdp", None), P("rep", "fsdp", None)),
        check_vma=False,
    )
```

```python
import jax
import jax.numpy as jnp
from jax import lax
from jax.experimental import pallas as pl
from jax.experimental.pallas import tpu as pltpu
from jax.sharding import PartitionSpec as P

NX, NH, NY = 4, 2, 4
N_PLANE = NX * NY
N_CHIP, N_CORE = 4, 2
N_FSDP = N_CHIP * N_CORE


def replica_at(spot, half):
    return (spot // NY * NH + half) * NY + spot % NY


PLANES = [[replica_at(spot, half) for spot in range(N_PLANE)] for half in range(NH)]
ACROSS = [
    (replica_at(spot, half), replica_at(spot, 1 - half))
    for spot in range(N_PLANE)
    for half in range(NH)
]


def between_chips(pairs):
    return [
        (src * N_CORE + core, dst * N_CORE + core) for src, dst in pairs for core in range(N_CORE)
    ]


ENDS_SWAP = between_chips([(0, 1), (1, 0), (2, 3), (3, 2)])
MID_SWAP = between_chips([(1, 2), (2, 1)])
MID_TO_ENDS = between_chips([(1, 0), (2, 3)])
SIBLING = [(i, i ^ 1) for i in range(N_FSDP)]


def chips_apart(step):
    return between_chips([(i, i ^ step) for i in range(N_CHIP)])


WIDTHS = (4, 6, 8, 10, 12, 16)


def by_chunks(ref, body):
    @pl.loop(0, ref.shape[0] // 16)
    def _(i):
        for col in range(0, ref.shape[1], 512):
            body((pl.ds(pl.multiple_of(i * 16, 16), 16), pl.ds(col, 512)))


def mixing_term(drift, w_slow):
    def kernel(drift_ref, slow_ref, out_ref):
        def chunk(at):
            out_ref[at] = (
                0.5
                * (
                    0.7 * drift_ref[at].astype(jnp.float32)
                    - 0.3 * slow_ref[at].astype(jnp.float32)
                )
            ).astype(jnp.bfloat16)

        by_chunks(out_ref, chunk)

    rows, cols = drift.shape
    tile = pl.BlockSpec((rows // 4, cols), lambda i: (i, 0))
    return pl.pallas_call(
        kernel,
        grid=(4,),
        out_shape=jax.ShapeDtypeStruct(drift.shape, drift.dtype),
        in_specs=[tile, tile],
        out_specs=tile,
        compiler_params=pltpu.CompilerParams(vmem_limit_bytes=14 << 20),
    )(drift, w_slow)


def route(held, moved, pick):
    def kernel(pick_ref, held_ref, moved_ref, out_ref, sems):
        for spot in range(N_PLANE):
            at = pick_ref[spot]

            @pl.when(at < N_PLANE)
            def _():
                pltpu.make_async_copy(
                    held_ref.at[jnp.minimum(at, N_PLANE - 1)], out_ref.at[spot], sems.at[spot]
                ).start()

            @pl.when(at >= N_PLANE)
            def _():
                from_far = jnp.clip(at - N_PLANE, 0, moved_ref.shape[0] - 1)
                pltpu.make_async_copy(
                    moved_ref.at[from_far], out_ref.at[spot], sems.at[spot]
                ).start()

        for spot in range(N_PLANE):
            pltpu.make_async_copy(held_ref.at[0], out_ref.at[spot], sems.at[spot]).wait()

    return pl.pallas_call(
        kernel,
        out_shape=jax.ShapeDtypeStruct(held.shape, held.dtype),
        in_specs=[
            pl.BlockSpec(memory_space=pltpu.SMEM),
            pl.BlockSpec(memory_space=pltpu.VMEM),
            pl.BlockSpec(memory_space=pltpu.VMEM),
        ],
        out_specs=pl.BlockSpec(memory_space=pl.ANY),
        scratch_shapes=[pltpu.SemaphoreType.DMA((N_PLANE,))],
        compiler_params=pltpu.CompilerParams(vmem_limit_bytes=14 << 20),
        cost_estimate=pl.CostEstimate(
            flops=0, bytes_accessed=200 * held.size, transcendentals=0
        ),
    )(pick, held, moved)


def plane_plan(partner, half):
    spots = jnp.arange(N_PLANE, dtype=jnp.int32)
    mate = partner[replica_at(spots, half)]
    mate_spot = mate // (NH * NY) * NY + mate % NY
    crosses = mate // NY % NH != half
    place = jnp.cumsum(crosses.astype(jnp.int32)) - 1
    return mate_spot, crosses, place


def in_plane(blocks):
    return lax.all_to_all(
        blocks, "rep", split_axis=0, concat_axis=0, tiled=True, axis_index_groups=PLANES
    )


def add_products(acc, pairs, square):
    rows, cols = pairs[0][0].shape[1], pairs[0][1].shape[1]
    tile = 1024
    flat = [part for pair in pairs for part in pair]
    n_acc = acc is not None

    def kernel(*refs):
        ins, outs = refs[: n_acc + len(flat)], refs[n_acc + len(flat) :]
        total = ins[0][...] if n_acc else None
        at = n_acc
        for x, *gs in pairs:
            g = ins[at + 1][...]
            for k in range(1, len(gs)):
                g = g + ins[at + 1 + k][...]
            part = lax.dot_general(
                ins[at][...], g, (((0,), (0,)), ((), ())), preferred_element_type=jnp.float32
            )
            total = part if total is None else total + part
            at += 1 + len(gs)
        outs[0][...] = total
        if square:
            sums = jnp.sum((total * total).reshape(rows // 8, 8, tile), axis=0)
            sums = sum(sums[:, k * 128 : (k + 1) * 128] for k in range(tile // 128))

            @pl.when(pl.program_id(0) == 0)
            def _():
                outs[1][...] = sums

            @pl.when(pl.program_id(0) > 0)
            def _():
                outs[1][...] += sums

    wide = pl.BlockSpec((rows, tile), lambda i: (0, i))
    specs = [wide] * n_acc
    for x, *gs in pairs:
        specs.append(pl.BlockSpec(x.shape, lambda i: (0, 0)))
        specs += [pl.BlockSpec((g.shape[0], tile), lambda i: (0, i)) for g in gs]
    out_shape = [jax.ShapeDtypeStruct((rows, cols), jnp.float32)]
    out_specs = [wide]
    if square:
        out_shape.append(jax.ShapeDtypeStruct((8, 128), jnp.float32))
        out_specs.append(pl.BlockSpec((8, 128), lambda i: (0, 0)))
    return pl.pallas_call(
        kernel,
        grid=(cols // tile,),
        out_shape=out_shape,
        in_specs=specs,
        out_specs=out_specs,
        compiler_params=pltpu.CompilerParams(vmem_limit_bytes=24 << 20),
        cost_estimate=pl.CostEstimate(
            flops=0,
            bytes_accessed=rows * cols,
            transcendentals=0,
        ),
    )(*([acc] if n_acc else []), *flat)


def elementwise(body, ins, outs, squares=()):
    n_ins, n_squares = len(ins), len(squares)

    def kernel(*refs):
        data, tiles = refs[:n_ins], refs[n_ins : n_ins + n_squares]
        out = refs[n_ins + n_squares :]
        extra = ()
        if n_squares:
            total = tiles[0][...]
            for ref in tiles[1:]:
                total = total + ref[...]
            total = jnp.sum(jnp.sum(total, axis=0, keepdims=True), axis=1, keepdims=True)
            extra = (total,)

        def chunk(at):
            results = body(*(ref[at].astype(jnp.float32) for ref in data), *extra)
            for ref, value in zip(out, results):
                ref[at] = value.astype(ref.dtype)

        by_chunks(data[0], chunk)

    rows, cols = ins[0].shape
    tile = pl.BlockSpec((rows // 4, cols), lambda i: (i, 0))
    whole = pl.BlockSpec((8, 128), lambda i: (0, 0))
    return pl.pallas_call(
        kernel,
        grid=(4,),
        out_shape=[jax.ShapeDtypeStruct((rows, cols), dtype) for dtype in outs],
        in_specs=[tile] * n_ins + [whole] * n_squares,
        out_specs=[tile] * len(outs),
        compiler_params=pltpu.CompilerParams(vmem_limit_bytes=14 << 20),
        cost_estimate=pl.CostEstimate(
            flops=8 * rows * cols, bytes_accessed=14 * rows * cols, transcendentals=0
        ),
    )(*ins, *squares)


def own_part(momentum, drift, w_slow):
    def body(momentum, drift, slow):
        part = 0.5 * momentum + 0.35 * drift + 0.15 * slow
        return part, slow - part

    return elementwise(body, (momentum, drift, w_slow), (jnp.float32, jnp.float32))


def momentum_step(part, mix):
    return elementwise(lambda part, mix: (part + mix,), (part, mix), (jnp.bfloat16,))[0]


def weight_step(rest, mix, grad, squares, count):
    def body(rest, mix, grad, total):
        factor = jnp.broadcast_to(0.5 / jnp.sqrt(total / count + 1e-06), grad.shape)
        return (rest - mix - grad * factor,)

    return elementwise(body, (rest, mix, grad), (jnp.bfloat16,), squares)[0]


def after(values, *arrays):
    def kernel(values_ref, *refs):
        for i in range(values.shape[0]):
            refs[-1][i] = values_ref[i]

    return pl.pallas_call(
        kernel,
        out_shape=jax.ShapeDtypeStruct(values.shape, values.dtype),
        in_specs=[pl.BlockSpec(memory_space=pltpu.SMEM)]
        + [pl.BlockSpec(memory_space=pl.ANY)] * len(arrays),
        out_specs=pl.BlockSpec(memory_space=pltpu.SMEM),
        cost_estimate=pl.CostEstimate(flops=3 * 10**9, bytes_accessed=0, transcendentals=0),
    )(values, *arrays)


def on_device(tokens, cotangent, w_slow, drift, momentum, partner):
    local_x, local_g = tokens[0], cotangent[0]
    rows, cols = w_slow.shape[1:]
    half = lax.axis_index("rep") // NY % NH
    me = lax.axis_index("fsdp")
    chip, core = me // N_CORE, me % N_CORE

    def hop(x, pairs):
        return lax.ppermute(x, "fsdp", pairs)

    def to_sibling(x):
        return hop(x, SIBLING)

    def columns_from(step):
        span = N_CORE * rows
        x = lax.dynamic_slice_in_dim(local_x, (chip ^ step) * span, span, axis=1)
        return hop(x, chips_apart(step)) if step else x

    def halves(x):
        own = lax.dynamic_slice_in_dim(x, core * rows, rows, axis=1)
        other = lax.dynamic_slice_in_dim(x, (1 - core) * rows, rows, axis=1)
        return own, to_sibling(other)

    mate_spot, crosses, place = plane_plan(partner, half)
    far_spot, far_crosses, far_place = plane_plan(partner, 1 - half)
    slots = jnp.arange(N_PLANE, dtype=jnp.int32)
    wanted = jnp.sum(
        jnp.where(
            far_crosses[None, :] & (far_place[None, :] == slots[:, None]), far_spot[None, :], 0
        ),
        axis=1,
    )
    pick = jnp.where(crosses, N_PLANE + place, mate_spot)
    count = jnp.sum(crosses.astype(jnp.int32))
    case = sum((count > width).astype(jnp.int32) for width in WIDTHS[:-1])
    g_near = hop(local_g, ENDS_SWAP)
    g_mid = hop(local_g, MID_SWAP)
    near_x = [columns_from(step) for step in range(3)]
    mix = mixing_term(drift[0], w_slow[0])
    held = in_plane(mix.reshape(N_PLANE, rows // N_PLANE, cols))
    wanted = after(wanted, g_near, g_mid, near_x[1], near_x[2])
    plan = (wanted, pick, case, own_part(momentum[0], drift[0], w_slow[0]))
    held, g_near, g_mid, near_x, plan = lax.optimization_barrier(
        (held, g_near, g_mid, near_x, plan)
    )
    wanted, pick, case, (part, rest) = plan

    g_ends = hop(g_mid, MID_TO_ENDS)
    g_far = hop(g_near, MID_SWAP)

    def cross(width):
        def branch(held):
            sent = jnp.take(held, wanted[:width], axis=0, mode="clip")
            routed = route(held, lax.ppermute(sent, "rep", ACROSS), pick)
            return routed

        return branch

    routed = lax.switch(
        case, [cross(width) for width in WIDTHS], held
    )

    g_last = hop(g_far, MID_TO_ENDS)
    last_x = [
        hop(
            lax.dynamic_slice_in_dim(local_x, (me ^ step) * rows, rows, axis=1),
            [(i, i ^ step) for i in range(N_FSDP)],
        )
        for step in (6, 7)
    ]
    partner_mix = in_plane(routed).reshape(rows, cols)
    xs = [halves(x) for x in near_x]
    (acc,) = add_products(
        None,
        [
            (xs[0][0], local_g),
            (xs[0][1], to_sibling(local_g)),
            (xs[1][0], g_near),
            (xs[1][1], to_sibling(g_near)),
            (xs[2][0], g_ends, g_far),
            (xs[2][1], to_sibling(g_ends), to_sibling(g_far)),
        ],
        False,
    )
    sib_mid = to_sibling(g_mid)
    g_last, last_x, acc, sib_mid = lax.optimization_barrier((g_last, last_x, acc, sib_mid))
    grad, squares = add_products(
        acc,
        [(last_x[0], g_mid, g_last), (last_x[1], sib_mid, to_sibling(g_last))],
        True,
    )
    squares = squares + to_sibling(squares)
    others = [hop(squares, chips_apart(step)) for step in (1, 2, 3)]
    moment = momentum_step(part, partner_mix)
    weights = weight_step(rest, partner_mix, grad, [squares] + others, rows * N_FSDP * cols)
    return (moment[None], weights[None])


def solution(mesh):
    return jax.shard_map(
        on_device,
        mesh=mesh,
        in_specs=(
            P("rep", "fsdp", None),
            P("rep", "fsdp", None),
            P("rep", "fsdp", None),
            P("rep", "fsdp", None),
            P("rep", "fsdp", None),
            P(),
        ),
        out_specs=(P("rep", "fsdp", None), P("rep", "fsdp", None)),
        check_vma=False,
    )
```

```python
import jax
import jax.numpy as jnp
from jax import lax
from jax.experimental import pallas as pl
from jax.experimental.pallas import tpu as pltpu
from jax.sharding import PartitionSpec as P

NX, NH, NY = 4, 2, 4
N_PLANE = NX * NY
N_CHIP, N_CORE = 4, 2
N_FSDP = N_CHIP * N_CORE


def replica_at(spot, half):
    return (spot // NY * NH + half) * NY + spot % NY


PLANES = [[replica_at(spot, half) for spot in range(N_PLANE)] for half in range(NH)]
ACROSS = [
    (replica_at(spot, half), replica_at(spot, 1 - half))
    for spot in range(N_PLANE)
    for half in range(NH)
]


def between_chips(pairs):
    return [
        (src * N_CORE + core, dst * N_CORE + core) for src, dst in pairs for core in range(N_CORE)
    ]


ENDS_SWAP = between_chips([(0, 1), (1, 0), (2, 3), (3, 2)])
MID_SWAP = between_chips([(1, 2), (2, 1)])
MID_TO_ENDS = between_chips([(1, 0), (2, 3)])
SIBLING = [(i, i ^ 1) for i in range(N_FSDP)]


def chips_apart(step):
    return between_chips([(i, i ^ step) for i in range(N_CHIP)])


WIDTHS = (4, 6, 8, 10, 12, 16)


def by_chunks(ref, body):
    @pl.loop(0, ref.shape[0] // 16)
    def _(i):
        for col in range(0, ref.shape[1], 512):
            body((pl.ds(pl.multiple_of(i * 16, 16), 16), pl.ds(col, 512)))


def mixing_term(drift, w_slow):
    def kernel(drift_ref, slow_ref, out_ref):
        def chunk(at):
            out_ref[at] = (
                0.5
                * (
                    0.7 * drift_ref[at].astype(jnp.float32)
                    - 0.3 * slow_ref[at].astype(jnp.float32)
                )
            ).astype(jnp.bfloat16)

        by_chunks(out_ref, chunk)

    rows, cols = drift.shape
    tile = pl.BlockSpec((rows // 4, cols), lambda i: (i, 0))
    return pl.pallas_call(
        kernel,
        grid=(4,),
        out_shape=jax.ShapeDtypeStruct(drift.shape, drift.dtype),
        in_specs=[tile, tile],
        out_specs=tile,
        compiler_params=pltpu.CompilerParams(vmem_limit_bytes=14 << 20),
    )(drift, w_slow)


def route(held, moved, pick):
    def kernel(pick_ref, held_ref, moved_ref, out_ref, sems):
        for spot in range(N_PLANE):
            at = pick_ref[spot]

            @pl.when(at < N_PLANE)
            def _():
                pltpu.make_async_copy(
                    held_ref.at[jnp.minimum(at, N_PLANE - 1)], out_ref.at[spot], sems.at[spot]
                ).start()

            @pl.when(at >= N_PLANE)
            def _():
                from_far = jnp.clip(at - N_PLANE, 0, moved_ref.shape[0] - 1)
                pltpu.make_async_copy(
                    moved_ref.at[from_far], out_ref.at[spot], sems.at[spot]
                ).start()

        for spot in range(N_PLANE):
            pltpu.make_async_copy(held_ref.at[0], out_ref.at[spot], sems.at[spot]).wait()

    return pl.pallas_call(
        kernel,
        out_shape=jax.ShapeDtypeStruct(held.shape, held.dtype),
        in_specs=[
            pl.BlockSpec(memory_space=pltpu.SMEM),
            pl.BlockSpec(memory_space=pltpu.VMEM),
            pl.BlockSpec(memory_space=pltpu.VMEM),
        ],
        out_specs=pl.BlockSpec(memory_space=pl.ANY),
        scratch_shapes=[pltpu.SemaphoreType.DMA((N_PLANE,))],
        compiler_params=pltpu.CompilerParams(vmem_limit_bytes=14 << 20),
        cost_estimate=pl.CostEstimate(
            flops=0, bytes_accessed=200 * held.size, transcendentals=0
        ),
    )(pick, held, moved)


def plane_plan(partner, half):
    spots = jnp.arange(N_PLANE, dtype=jnp.int32)
    mate = partner[replica_at(spots, half)]
    mate_spot = mate // (NH * NY) * NY + mate % NY
    crosses = mate // NY % NH != half
    place = jnp.cumsum(crosses.astype(jnp.int32)) - 1
    return mate_spot, crosses, place


def in_plane(blocks):
    return lax.all_to_all(
        blocks, "rep", split_axis=0, concat_axis=0, tiled=True, axis_index_groups=PLANES
    )


def add_products(acc, pairs, square):
    rows, cols = pairs[0][0].shape[1], pairs[0][1].shape[1]
    tile = 1024
    flat = [part for pair in pairs for part in pair]
    n_acc = acc is not None

    def kernel(*refs):
        ins, outs = refs[: n_acc + len(flat)], refs[n_acc + len(flat) :]
        total = ins[0][...] if n_acc else None
        at = n_acc
        for x, *gs in pairs:
            g = ins[at + 1][...]
            for k in range(1, len(gs)):
                g = g + ins[at + 1 + k][...]
            part = lax.dot_general(
                ins[at][...], g, (((0,), (0,)), ((), ())), preferred_element_type=jnp.float32
            )
            total = part if total is None else total + part
            at += 1 + len(gs)
        outs[0][...] = total
        if square:
            sums = jnp.sum((total * total).reshape(rows // 8, 8, tile), axis=0)
            sums = sum(sums[:, k * 128 : (k + 1) * 128] for k in range(tile // 128))

            @pl.when(pl.program_id(0) == 0)
            def _():
                outs[1][...] = sums

            @pl.when(pl.program_id(0) > 0)
            def _():
                outs[1][...] += sums

    wide = pl.BlockSpec((rows, tile), lambda i: (0, i))
    specs = [wide] * n_acc
    for x, *gs in pairs:
        specs.append(pl.BlockSpec(x.shape, lambda i: (0, 0)))
        specs += [pl.BlockSpec((g.shape[0], tile), lambda i: (0, i)) for g in gs]
    out_shape = [jax.ShapeDtypeStruct((rows, cols), jnp.float32)]
    out_specs = [wide]
    if square:
        out_shape = [pltpu.HBM((rows, cols), jnp.float32)]
        out_shape.append(jax.ShapeDtypeStruct((8, 128), jnp.float32))
        out_specs.append(pl.BlockSpec((8, 128), lambda i: (0, 0)))
    return pl.pallas_call(
        kernel,
        grid=(cols // tile,),
        out_shape=out_shape,
        in_specs=specs,
        out_specs=out_specs,
        compiler_params=pltpu.CompilerParams(vmem_limit_bytes=24 << 20),
        cost_estimate=pl.CostEstimate(
            flops=0,
            bytes_accessed=rows * cols,
            transcendentals=0,
        ),
    )(*([acc] if n_acc else []), *flat)


def elementwise(body, ins, outs, squares=()):
    n_ins, n_squares = len(ins), len(squares)

    def kernel(*refs):
        data, tiles = refs[:n_ins], refs[n_ins : n_ins + n_squares]
        out = refs[n_ins + n_squares :]
        extra = ()
        if n_squares:
            total = tiles[0][...]
            for ref in tiles[1:]:
                total = total + ref[...]
            total = jnp.sum(jnp.sum(total, axis=0, keepdims=True), axis=1, keepdims=True)
            extra = (total,)

        def chunk(at):
            results = body(*(ref[at].astype(jnp.float32) for ref in data), *extra)
            for ref, value in zip(out, results):
                ref[at] = value.astype(ref.dtype)

        by_chunks(data[0], chunk)

    rows, cols = ins[0].shape
    tile = pl.BlockSpec((rows // 4, cols), lambda i: (i, 0))
    whole = pl.BlockSpec((8, 128), lambda i: (0, 0))
    return pl.pallas_call(
        kernel,
        grid=(4,),
        out_shape=[jax.ShapeDtypeStruct((rows, cols), dtype) for dtype in outs],
        in_specs=[tile] * n_ins + [whole] * n_squares,
        out_specs=[tile] * len(outs),
        compiler_params=pltpu.CompilerParams(vmem_limit_bytes=14 << 20),
        cost_estimate=pl.CostEstimate(
            flops=8 * rows * cols, bytes_accessed=14 * rows * cols, transcendentals=0
        ),
    )(*ins, *squares)


def own_part(momentum, drift, w_slow):
    def body(momentum, drift, slow):
        part = 0.5 * momentum + 0.35 * drift + 0.15 * slow
        return part, slow - part

    return elementwise(body, (momentum, drift, w_slow), (jnp.float32, jnp.float32))


def momentum_step(part, mix):
    return elementwise(lambda part, mix: (part + mix,), (part, mix), (jnp.bfloat16,))[0]


def weight_step(rest, mix, grad, squares, count):
    def body(rest, mix, grad, total):
        factor = jnp.broadcast_to(0.5 / jnp.sqrt(total / count + 1e-06), grad.shape)
        return (rest - mix - grad * factor,)

    return elementwise(body, (rest, mix, grad), (jnp.bfloat16,), squares)[0]


def after(values, *arrays):
    def kernel(values_ref, *refs):
        for i in range(values.shape[0]):
            refs[-1][i] = values_ref[i]

    return pl.pallas_call(
        kernel,
        out_shape=jax.ShapeDtypeStruct(values.shape, values.dtype),
        in_specs=[pl.BlockSpec(memory_space=pltpu.SMEM)]
        + [pl.BlockSpec(memory_space=pl.ANY)] * len(arrays),
        out_specs=pl.BlockSpec(memory_space=pltpu.SMEM),
        cost_estimate=pl.CostEstimate(flops=3 * 10**9, bytes_accessed=0, transcendentals=0),
    )(values, *arrays)


def on_device(tokens, cotangent, w_slow, drift, momentum, partner):
    local_x, local_g = tokens[0], cotangent[0]
    rows, cols = w_slow.shape[1:]
    half = lax.axis_index("rep") // NY % NH
    me = lax.axis_index("fsdp")
    chip, core = me // N_CORE, me % N_CORE

    def hop(x, pairs):
        return lax.ppermute(x, "fsdp", pairs)

    def to_sibling(x):
        return hop(x, SIBLING)

    def columns_from(step):
        span = N_CORE * rows
        x = lax.dynamic_slice_in_dim(local_x, (chip ^ step) * span, span, axis=1)
        return hop(x, chips_apart(step)) if step else x

    def halves(x):
        own = lax.dynamic_slice_in_dim(x, core * rows, rows, axis=1)
        other = lax.dynamic_slice_in_dim(x, (1 - core) * rows, rows, axis=1)
        return own, to_sibling(other)

    mate_spot, crosses, place = plane_plan(partner, half)
    far_spot, far_crosses, far_place = plane_plan(partner, 1 - half)
    slots = jnp.arange(N_PLANE, dtype=jnp.int32)
    wanted = jnp.sum(
        jnp.where(
            far_crosses[None, :] & (far_place[None, :] == slots[:, None]), far_spot[None, :], 0
        ),
        axis=1,
    )
    pick = jnp.where(crosses, N_PLANE + place, mate_spot)
    count = jnp.sum(crosses.astype(jnp.int32))
    case = sum((count > width).astype(jnp.int32) for width in WIDTHS[:-1])
    g_near = hop(local_g, ENDS_SWAP)
    g_mid = hop(local_g, MID_SWAP)
    near_x = [columns_from(step) for step in range(3)]
    mix = mixing_term(drift[0], w_slow[0])
    held = in_plane(mix.reshape(N_PLANE, rows // N_PLANE, cols))
    wanted = after(wanted, g_near, g_mid, near_x[1], near_x[2])
    plan = (wanted, pick, case, own_part(momentum[0], drift[0], w_slow[0]))
    held, g_near, g_mid, near_x, plan = lax.optimization_barrier(
        (held, g_near, g_mid, near_x, plan)
    )
    wanted, pick, case, (part, rest) = plan

    g_ends = hop(g_mid, MID_TO_ENDS)
    g_far = hop(g_near, MID_SWAP)

    def cross(width):
        def branch(held):
            sent = jnp.take(held, wanted[:width], axis=0, mode="clip")
            routed = route(held, lax.ppermute(sent, "rep", ACROSS), pick)
            return routed

        return branch

    routed = lax.switch(
        case, [cross(width) for width in WIDTHS], held
    )

    g_last = hop(g_far, MID_TO_ENDS)
    last_x = [
        hop(
            lax.dynamic_slice_in_dim(local_x, (me ^ step) * rows, rows, axis=1),
            [(i, i ^ step) for i in range(N_FSDP)],
        )
        for step in (6, 7)
    ]
    partner_mix = in_plane(routed).reshape(rows, cols)
    xs = [halves(x) for x in near_x]
    (acc,) = add_products(
        None,
        [
            (xs[0][0], local_g),
            (xs[0][1], to_sibling(local_g)),
            (xs[1][0], g_near),
            (xs[1][1], to_sibling(g_near)),
            (xs[2][0], g_ends, g_far),
            (xs[2][1], to_sibling(g_ends), to_sibling(g_far)),
        ],
        False,
    )
    sib_mid = to_sibling(g_mid)
    g_last, last_x, acc, sib_mid = lax.optimization_barrier((g_last, last_x, acc, sib_mid))
    grad, squares = add_products(
        acc,
        [(last_x[0], g_mid, g_last), (last_x[1], sib_mid, to_sibling(g_last))],
        True,
    )
    squares = squares + to_sibling(squares)
    others = [hop(squares, chips_apart(step)) for step in (1, 2, 3)]
    moment = momentum_step(part, partner_mix)
    weights = weight_step(rest, partner_mix, grad, [squares] + others, rows * N_FSDP * cols)
    return (moment[None], weights[None])


def solution(mesh):
    return jax.shard_map(
        on_device,
        mesh=mesh,
        in_specs=(
            P("rep", "fsdp", None),
            P("rep", "fsdp", None),
            P("rep", "fsdp", None),
            P("rep", "fsdp", None),
            P("rep", "fsdp", None),
            P(),
        ),
        out_specs=(P("rep", "fsdp", None), P("rep", "fsdp", None)),
        check_vma=False,
    )
```
